512 devices in a mesh: space: 64 (over x, z, core), tm: 8 (over y).
Axes of the slice: x: 4, y: 8, z: 8, core: 2. Of those that a mesh axis runs over, the one named last changes fastest.
Arguments:
- thermal_anomaly: bfloat16 [512, 561152], P('tm', 'space'), may hold values from -6 to 6
- smoothing_coefs: float32 [128], replicated, may hold values from -0.0075 to 0.0075
Outputs:
- orthonormal_basis: float32 [512, 561152], P(None, ('space', 'tm'))
- triangular_factor: float32 [512, 512], replicated
The draws below stay inside these ranges and needn't reach their ends.
All inputs are finite; a program needn't handle non-finite values.
Results may differ from the reference program's by a relative error of at most 0.0003.
The reference program's roundings to bfloat16 on the way count: a program that leaves them out, or rounds other values in their place, can miss the bound.
Values may be sent and summed in bfloat16 or wider, within the bound.
No kernel may reach another device: no remote copies, remote signals or barrier semaphores. Data moves between devices by JAX's collectives and lax.ppermute only.
A program may use at most 64 MiB of HBM per device.

```python
import math
import jax
import jax.numpy as jnp
from jax import lax

TAPS = 129
SPAN_TIMESTEPS = 512
SPATIAL_SITES = 561152


def draw_thermal_anomaly(key, part):
    keys = jax.random.split(jax.random.fold_in(key, 17), 5)
    count = 6
    hours = jnp.arange(SPAN_TIMESTEPS, dtype=jnp.float32)[:, None]
    cycles = jax.random.uniform(keys[0], (count,), jnp.float32, 0.5, 8.0)
    phases = jax.random.uniform(keys[1], (count,), jnp.float32, -math.pi, math.pi)
    root_three = math.sqrt(3.0)
    patterns = jax.random.uniform(keys[3], (count, SPATIAL_SITES), jnp.float32, -root_three, root_three)
    strengths = jnp.exp(jax.random.uniform(keys[2], (count,), jnp.float32, math.log(0.12), math.log(0.35)))
    noise = jax.random.truncated_normal(keys[4], -3.0, 3.0, (SPAN_TIMESTEPS, SPATIAL_SITES), jnp.float32)
    total = noise
    for index in range(count):
        temporal = math.sqrt(2.0) * jnp.cos(2.0 * math.pi * cycles[index] * hours / SPAN_TIMESTEPS + phases[index])
        total = total + strengths[index] * temporal * patterns[index][None, :]
    return jnp.clip(total, -6.0, 6.0).astype(jnp.bfloat16)


def setup_inputs(seed: int = 0) -> dict:
    key_list = jax.random.split(jax.random.key(seed), 3)
    thermal_anomaly = draw_thermal_anomaly(jax.random.fold_in(key_list[2], 71), 0)
    smoothing_coefs = jnp.clip(jax.random.uniform(key_list[1], (TAPS - 1,), jnp.float32, -0.0075, 0.0075), -0.0075, 0.0075)
    return dict(thermal_anomaly=thermal_anomaly, smoothing_coefs=smoothing_coefs)


def banded_matrix(coefficients, count_rows, count_cols, delay_shift_amount):
    row_index = lax.broadcasted_iota(jnp.int32, (count_rows, count_cols), 0)
    col_index = lax.broadcasted_iota(jnp.int32, (count_rows, count_cols), 1)
    lag_index = row_index + delay_shift_amount - col_index
    length = coefficients.shape[0]
    inside = (lag_index >= 0) & (lag_index < length)
    safe = jnp.clip(lag_index, 0, length - 1).astype(jnp.int32)
    return jnp.where(inside, coefficients[safe], jnp.zeros((), coefficients.dtype))

def reference(thermal_anomaly, smoothing_coefs):
    coefficients = jnp.concatenate([jnp.ones((1,), jnp.float32), smoothing_coefs.astype(jnp.float32)]).astype(jnp.bfloat16)
    snapshot_array = banded_matrix(coefficients, SPAN_TIMESTEPS, SPAN_TIMESTEPS, 0)
    averaged_record = jnp.dot(snapshot_array.astype(jnp.float32), thermal_anomaly.astype(jnp.float32), preferred_element_type=jnp.float32).astype(jnp.bfloat16)
    gram = jnp.dot(averaged_record.astype(jnp.float32), averaged_record.T.astype(jnp.float32), preferred_element_type=jnp.float32)
    lower_one = jnp.linalg.cholesky(gram)
    first_rows = jax.scipy.linalg.solve_triangular(lower_one, averaged_record.astype(jnp.float32), lower=True)
    scale = jnp.sqrt(jnp.float32(SPATIAL_SITES))
    return (first_rows * scale, lower_one / scale)
```

```python
import functools
import math

import jax
import jax.numpy as jnp
from jax import lax
from jax.experimental import pallas as pl
from jax.experimental.pallas import tpu as pltpu
from jax.sharding import Mesh, PartitionSpec as P

BLOCK = 128
PANEL = 16
VMEM_BYTES = 48 * 2**20


def dot_exact(left, right, contract_left):
    return lax.dot_general(
        left,
        right,
        (((contract_left,), (0,)), ((), ())),
        precision=lax.Precision.HIGHEST,
        preferred_element_type=jnp.float32,
    )


def block_pairs(blocks):
    return [(i, j) for i in range(blocks) for j in range(i, blocks)]


def filter_kernel(taps_ref, hours_ref, filtered_ref, gram_ref):
    blocks = hours_ref.shape[0] // BLOCK
    band = pltpu.roll(
        jnp.broadcast_to(taps_ref[...], (BLOCK, 2 * BLOCK)), 0, 1, stride=1, stride_axis=0
    ).astype(jnp.bfloat16)
    for i in range(blocks):
        if i == 0:
            total = jnp.dot(
                band[:, BLOCK:], hours_ref[:BLOCK, :], preferred_element_type=jnp.float32
            )
        else:
            total = jnp.dot(
                band,
                hours_ref[(i - 1) * BLOCK : (i + 1) * BLOCK, :],
                preferred_element_type=jnp.float32,
            )
        filtered_ref[i * BLOCK : (i + 1) * BLOCK, :] = total.astype(jnp.bfloat16)
    place = 0
    for i in range(blocks):
        product = lax.dot_general(
            filtered_ref[i * BLOCK : (i + 1) * BLOCK, :],
            filtered_ref[i * BLOCK :, :],
            (((1,), (1,)), ((), ())),
            preferred_element_type=jnp.float32,
        )
        for j in range(blocks - i):
            gram_ref[place : place + BLOCK, :] = product[:, j * BLOCK : (j + 1) * BLOCK]
            place += BLOCK


def filtered_and_gram(hours, coefs):
    taps = jnp.concatenate(
        [coefs[::-1], jnp.ones((1,), jnp.float32), jnp.zeros((BLOCK - 1,), jnp.float32)]
    )
    count = hours.shape[0]
    pairs = len(block_pairs(count // BLOCK))
    return pl.pallas_call(
        filter_kernel,
        out_shape=[
            jax.ShapeDtypeStruct(hours.shape, jnp.bfloat16),
            jax.ShapeDtypeStruct((pairs * BLOCK, BLOCK), jnp.float32),
        ],
        compiler_params=pltpu.CompilerParams(vmem_limit_bytes=VMEM_BYTES),
    )(taps.reshape(1, 2 * BLOCK), hours)


def eliminate(rows, first):
    count = 8 * len(rows)
    sublane = lax.broadcasted_iota(jnp.int32, (8, 1), 0)
    columns = [
        [jnp.broadcast_to(tile[:, first + k : first + k + 1], (8, BLOCK)) for tile in rows]
        for k in range(count)
    ]
    rows = list(rows)
    for j in range(count):
        home, row = divmod(j, 8)
        inverse = lax.rsqrt(columns[j][home][row : row + 1])
        factors = [columns[j][t] * inverse if t >= home else None for t in range(len(rows))]
        for k in range(j + 1, count):
            line = columns[k][home][row : row + 1] * inverse
            for t in range(home, len(rows)):
                columns[k][t] = columns[k][t] - factors[t] * line
        line = rows[home][row : row + 1] * jnp.concatenate([inverse, inverse], 1)
        for t in range(home, len(rows)):
            factor = jnp.concatenate([factors[t], factors[t]], 1)
            if t == home:
                below = jnp.where(sublane > row, factor, 0.0)
                rows[t] = jnp.where(sublane == row, line, rows[t] - below * line)
            else:
                rows[t] = rows[t] - factor * line
    return rows


def factor_block(work):
    tiles = PANEL // 8
    for p in range(0, BLOCK, PANEL):
        rows = eliminate([work[p + 8 * t : p + 8 * t + 8, :] for t in range(tiles)], p)
        for t in range(tiles):
            work[p + 8 * t : p + 8 * t + 8, :] = rows[t]
        if p + PANEL < BLOCK:
            panel = jnp.concatenate(rows, 0)
            update = dot_exact(panel[:, :BLOCK], panel, 0)
            work[p + PANEL :, :] = work[p + PANEL :, :] - update[p + PANEL :]


def basis_kernel(scale, gram_ref, filtered_ref, basis_ref, lower_ref, rest, upper, inverse, work, points):
    count = filtered_ref.shape[0]
    blocks = count // BLOCK
    row = lax.broadcasted_iota(jnp.int32, (BLOCK, BLOCK), 0)
    column = lax.broadcasted_iota(jnp.int32, (BLOCK, BLOCK), 1)
    identity = (row == column).astype(jnp.float32)
    for place, (i, j) in enumerate(block_pairs(blocks)):
        rest[i * BLOCK : (i + 1) * BLOCK, j * BLOCK : (j + 1) * BLOCK] = gram_ref[
            place * BLOCK : (place + 1) * BLOCK, :
        ]
    lower_ref[...] = jnp.zeros_like(lower_ref)
    inverse[...] = jnp.zeros_like(inverse)
    for k in range(blocks):
        start, end = k * BLOCK, (k + 1) * BLOCK
        work[:, :BLOCK] = rest[start:end, start:end]
        work[:, BLOCK:] = identity
        factor_block(work)
        corner = work[:, BLOCK:]
        inverse[start:end, start:end] = corner
        lower_ref[start:end, start:end] = (
            jnp.where(row <= column, work[:, :BLOCK], 0.0) / scale
        ).T
        if k + 1 < blocks:
            across = dot_exact(corner, rest[start:end, end:], 1)
            upper[start:end, end:] = across
            lower_ref[end:, start:end] = (across / scale).T
            for i in range(k + 1, blocks):
                here = slice(i * BLOCK, (i + 1) * BLOCK)
                rest[here, i * BLOCK :] = rest[here, i * BLOCK :] - dot_exact(
                    across[:, (i - k - 1) * BLOCK : (i - k) * BLOCK],
                    across[:, (i - k - 1) * BLOCK :],
                    0,
                )
        if k > 0:
            inner = dot_exact(upper[:start, start:end], inverse[:start, :start], 0)
            inverse[start:end, :start] = -dot_exact(corner, inner, 1)
        left = inverse[start:end, :end] * scale
        points[:, start:end] = filtered_ref[start:end, :].T
        total = None
        for _ in range(3):
            part = left.astype(jnp.bfloat16)
            left = left - part.astype(jnp.float32)
            term = lax.dot_general(
                points[:, :end],
                part,
                (((1,), (1,)), ((), ())),
                preferred_element_type=jnp.float32,
            )
            total = term if total is None else total + term
        basis_ref[:, start:end] = total


def basis_and_factor(gram, filtered, scale):
    count = filtered.shape[0]
    square = (count, count)
    return pl.pallas_call(
        functools.partial(basis_kernel, scale),
        out_shape=[
            jax.ShapeDtypeStruct(filtered.shape[::-1], jnp.float32),
            jax.ShapeDtypeStruct(square, jnp.float32),
        ],
        scratch_shapes=[
            pltpu.VMEM(square, jnp.float32),
            pltpu.VMEM(square, jnp.float32),
            pltpu.VMEM(square, jnp.float32),
            pltpu.VMEM((BLOCK, 2 * BLOCK), jnp.float32),
            pltpu.VMEM(filtered.shape[::-1], jnp.bfloat16),
        ],
        compiler_params=pltpu.CompilerParams(vmem_limit_bytes=VMEM_BYTES),
    )(gram, filtered)


def exchanged(parts, axes):
    return lax.all_to_all(parts, axes, split_axis=0, concat_axis=0, tiled=True)


def total_gram(gram):
    plane, line = ("x", "z"), ("core", "tm")
    count_plane, count_line = lax.axis_size(plane), lax.axis_size(line)
    each = gram.shape[0] // count_plane
    pieces = exchanged(gram, plane).reshape(count_plane, each, BLOCK)
    piece = jnp.sum(pieces, 0)
    copies = jnp.broadcast_to(piece[None], (count_line, each, BLOCK))
    sums = exchanged(copies.reshape(count_line * each, BLOCK), line)
    piece = jnp.sum(sums.reshape(count_line, each, BLOCK), 0)
    copies = jnp.broadcast_to(piece[None], (count_plane, each, BLOCK))
    return exchanged(copies.reshape(count_plane * each, BLOCK), plane)


def body(thermal_anomaly, smoothing_coefs):
    points = thermal_anomaly.shape[1] * lax.axis_size(("x", "z", "core"))
    scale = math.sqrt(points)
    hours = lax.all_to_all(thermal_anomaly, "tm", split_axis=1, concat_axis=0, tiled=True)
    filtered, gram = filtered_and_gram(hours, smoothing_coefs)
    basis, lower = basis_and_factor(total_gram(gram), filtered, scale)
    return basis.T, lower


def solution(mesh):
    fine = Mesh(mesh.devices.reshape(4, 8, 2, 8), ("x", "z", "core", "tm"))
    space = ("x", "z", "core")
    return jax.shard_map(
        body,
        mesh=fine,
        in_specs=(P("tm", space), P()),
        out_specs=(P(None, space + ("tm",)), P()),
        check_vma=False,
    )
```

```python
import functools
import math

import jax
import jax.numpy as jnp
from jax import lax
from jax.experimental import pallas as pl
from jax.experimental.pallas import tpu as pltpu
from jax.sharding import Mesh, PartitionSpec as P

BLOCK = 128
PANEL = 16
VMEM_BYTES = 48 * 2**20


def dot_exact(left, right, contract_left):
    def parts(value):
        found = []
        for _ in range(3):
            part = value.astype(jnp.bfloat16)
            value = value - part.astype(jnp.float32)
            found.append(part)
        return found

    lefts, rights = parts(left), parts(right)
    pairs = ((0, 0), (0, 1), (1, 0), (0, 2), (2, 0), (1, 1))
    return lax.dot_general(
        jnp.concatenate([lefts[i] for i, _ in pairs], contract_left),
        jnp.concatenate([rights[j] for _, j in pairs], 0),
        (((contract_left,), (0,)), ((), ())),
        preferred_element_type=jnp.float32,
    )


def block_pairs(blocks):
    return [(i, j) for i in range(blocks) for j in range(i, blocks)]


def filter_kernel(taps_ref, hours_ref, filtered_ref, gram_ref):
    blocks = hours_ref.shape[0] // BLOCK
    band = pltpu.roll(
        jnp.broadcast_to(taps_ref[...], (BLOCK, 2 * BLOCK)), 0, 1, stride=1, stride_axis=0
    ).astype(jnp.bfloat16)
    for i in range(blocks):
        if i == 0:
            total = jnp.dot(
                band[:, BLOCK:], hours_ref[:BLOCK, :], preferred_element_type=jnp.float32
            )
        else:
            total = jnp.dot(
                band,
                hours_ref[(i - 1) * BLOCK : (i + 1) * BLOCK, :],
                preferred_element_type=jnp.float32,
            )
        filtered_ref[i * BLOCK : (i + 1) * BLOCK, :] = total.astype(jnp.bfloat16)
    place = 0
    for i in range(blocks):
        product = lax.dot_general(
            filtered_ref[i * BLOCK : (i + 1) * BLOCK, :],
            filtered_ref[i * BLOCK :, :],
            (((1,), (1,)), ((), ())),
            preferred_element_type=jnp.float32,
        )
        for j in range(blocks - i):
            gram_ref[place : place + BLOCK, :] = product[:, j * BLOCK : (j + 1) * BLOCK]
            place += BLOCK


def filtered_and_gram(hours, coefs):
    taps = jnp.concatenate(
        [coefs[::-1], jnp.ones((1,), jnp.float32), jnp.zeros((BLOCK - 1,), jnp.float32)]
    )
    count = hours.shape[0]
    pairs = len(block_pairs(count // BLOCK))
    return pl.pallas_call(
        filter_kernel,
        out_shape=[
            jax.ShapeDtypeStruct(hours.shape, jnp.bfloat16),
            jax.ShapeDtypeStruct((pairs * BLOCK, BLOCK), jnp.float32),
        ],
        compiler_params=pltpu.CompilerParams(vmem_limit_bytes=VMEM_BYTES),
    )(taps.reshape(1, 2 * BLOCK), hours)


def eliminate(rows, first):
    count = 8 * len(rows)
    sublane = lax.broadcasted_iota(jnp.int32, (8, 1), 0)
    columns = [
        [jnp.broadcast_to(tile[:, first + k : first + k + 1], (8, BLOCK)) for tile in rows]
        for k in range(count)
    ]
    rows = list(rows)
    for j in range(count):
        home, row = divmod(j, 8)
        inverse = lax.rsqrt(columns[j][home][row : row + 1])
        factors = [columns[j][t] * inverse if t >= home else None for t in range(len(rows))]
        for k in range(j + 1, count):
            line = columns[k][home][row : row + 1] * inverse
            for t in range(home, len(rows)):
                columns[k][t] = columns[k][t] - factors[t] * line
        line = rows[home][row : row + 1] * jnp.concatenate([inverse, inverse], 1)
        for t in range(home, len(rows)):
            factor = jnp.concatenate([factors[t], factors[t]], 1)
            if t == home:
                below = jnp.where(sublane > row, factor, 0.0)
                rows[t] = jnp.where(sublane == row, line, rows[t] - below * line)
            else:
                rows[t] = rows[t] - factor * line
    return rows


def factor_block(work):
    tiles = PANEL // 8
    for p in range(0, BLOCK, PANEL):
        rows = eliminate([work[p + 8 * t : p + 8 * t + 8, :] for t in range(tiles)], p)
        for t in range(tiles):
            work[p + 8 * t : p + 8 * t + 8, :] = rows[t]
        if p + PANEL < BLOCK:
            panel = jnp.concatenate(rows, 0)
            update = dot_exact(panel[:, :BLOCK], panel, 0)
            work[p + PANEL :, :] = work[p + PANEL :, :] - update[p + PANEL :]


def basis_kernel(scale, gram_ref, filtered_ref, basis_ref, lower_ref, rest, upper, inverse, work, points):
    count = filtered_ref.shape[0]
    blocks = count // BLOCK
    row = lax.broadcasted_iota(jnp.int32, (BLOCK, BLOCK), 0)
    column = lax.broadcasted_iota(jnp.int32, (BLOCK, BLOCK), 1)
    identity = (row == column).astype(jnp.float32)
    for place, (i, j) in enumerate(block_pairs(blocks)):
        rest[i * BLOCK : (i + 1) * BLOCK, j * BLOCK : (j + 1) * BLOCK] = gram_ref[
            place * BLOCK : (place + 1) * BLOCK, :
        ]
    lower_ref[...] = jnp.zeros_like(lower_ref)
    inverse[...] = jnp.zeros_like(inverse)
    for k in range(blocks):
        start, end = k * BLOCK, (k + 1) * BLOCK
        work[:, :BLOCK] = rest[start:end, start:end]
        work[:, BLOCK:] = identity
        factor_block(work)
        corner = work[:, BLOCK:]
        inverse[start:end, start:end] = corner
        lower_ref[start:end, start:end] = (
            jnp.where(row <= column, work[:, :BLOCK], 0.0) / scale
        ).T
        if k + 1 < blocks:
            across = dot_exact(corner, rest[start:end, end:], 1)
            upper[start:end, end:] = across
            lower_ref[end:, start:end] = (across / scale).T
            for i in range(k + 1, blocks):
                here = slice(i * BLOCK, (i + 1) * BLOCK)
                rest[here, i * BLOCK :] = rest[here, i * BLOCK :] - dot_exact(
                    across[:, (i - k - 1) * BLOCK : (i - k) * BLOCK],
                    across[:, (i - k - 1) * BLOCK :],
                    0,
                )
        if k > 0:
            inner = dot_exact(upper[:start, start:end], inverse[:start, :start], 0)
            inverse[start:end, :start] = -dot_exact(corner, inner, 1)
        left = inverse[start:end, :end] * scale
        points[:, start:end] = filtered_ref[start:end, :].T
        total = None
        for _ in range(3):
            part = left.astype(jnp.bfloat16)
            left = left - part.astype(jnp.float32)
            term = lax.dot_general(
                points[:, :end],
                part,
                (((1,), (1,)), ((), ())),
                preferred_element_type=jnp.float32,
            )
            total = term if total is None else total + term
        basis_ref[:, start:end] = total


def basis_and_factor(gram, filtered, scale):
    count = filtered.shape[0]
    square = (count, count)
    return pl.pallas_call(
        functools.partial(basis_kernel, scale),
        out_shape=[
            jax.ShapeDtypeStruct(filtered.shape[::-1], jnp.float32),
            jax.ShapeDtypeStruct(square, jnp.float32),
        ],
        scratch_shapes=[
            pltpu.VMEM(square, jnp.float32),
            pltpu.VMEM(square, jnp.float32),
            pltpu.VMEM(square, jnp.float32),
            pltpu.VMEM((BLOCK, 2 * BLOCK), jnp.float32),
            pltpu.VMEM(filtered.shape[::-1], jnp.bfloat16),
        ],
        compiler_params=pltpu.CompilerParams(vmem_limit_bytes=VMEM_BYTES),
    )(gram, filtered)


def split_kernel(hours_ref, parts_ref):
    count, width = hours_ref.shape[0], parts_ref.shape[1]
    for part in range(parts_ref.shape[0] // count):
        parts_ref[part * count : (part + 1) * count, :] = hours_ref[
            :, part * width : (part + 1) * width
        ]


def split_points(hours, parts):
    count, width = hours.shape[0], hours.shape[1] // parts
    return pl.pallas_call(
        split_kernel,
        out_shape=jax.ShapeDtypeStruct((parts * count, width), hours.dtype),
        compiler_params=pltpu.CompilerParams(vmem_limit_bytes=VMEM_BYTES),
    )(hours)


def exchanged(parts, axes):
    return lax.all_to_all(parts, axes, split_axis=0, concat_axis=0, tiled=True)


def scattered_sum(parts, axes):
    count = lax.axis_size(axes)
    return jnp.sum(exchanged(parts, axes).reshape(count, -1, BLOCK), 0)


def gathered(piece, axes):
    count = lax.axis_size(axes)
    copies = jnp.broadcast_to(piece[None], (count,) + piece.shape)
    return exchanged(copies.reshape(-1, BLOCK), axes)


def swapped(piece):
    return lax.ppermute(piece, "core", [(0, 1), (1, 0)])


def total_gram(gram):
    core, half = lax.axis_index("core"), gram.shape[0] // 2
    own = lax.dynamic_slice_in_dim(gram, core * half, half)
    other = lax.dynamic_slice_in_dim(gram, (1 - core) * half, half)
    piece = scattered_sum(own + swapped(other), ("x", "z"))
    piece = jnp.sum(gathered(piece, "tm").reshape((-1,) + piece.shape), 0)
    own = gathered(piece, ("x", "z"))
    other = swapped(own)
    first = core == 0
    return jnp.concatenate([jnp.where(first, own, other), jnp.where(first, other, own)], 0)


def body(thermal_anomaly, smoothing_coefs):
    points = thermal_anomaly.shape[1] * lax.axis_size(("x", "z", "core"))
    scale = math.sqrt(points)
    hours = exchanged(split_points(thermal_anomaly, lax.axis_size("tm")), "tm")
    filtered, gram = filtered_and_gram(hours, smoothing_coefs)
    basis, lower = basis_and_factor(total_gram(gram), filtered, scale)
    return basis.T, lower


def solution(mesh):
    fine = Mesh(mesh.devices.reshape(4, 8, 2, 8), ("x", "z", "core", "tm"))
    space = ("x", "z", "core")
    return jax.shard_map(
        body,
        mesh=fine,
        in_specs=(P("tm", space), P()),
        out_specs=(P(None, space + ("tm",)), P()),
        check_vma=False,
    )
```

```python
import functools
import math

import jax
import jax.numpy as jnp
from jax import lax
from jax.experimental import pallas as pl
from jax.experimental.pallas import tpu as pltpu
from jax.sharding import Mesh, PartitionSpec as P

BLOCK = 128
PANEL = 32
VMEM_BYTES = 48 * 2**20


def parts_of(value):
    found = []
    for _ in range(3):
        part = value.astype(jnp.bfloat16)
        value = value - part.astype(jnp.float32)
        found.append(part)
    return found


def dot_parts(lefts, rights, contract_left):
    pairs = ((0, 0), (0, 1), (1, 0), (0, 2), (2, 0), (1, 1))
    return lax.dot_general(
        jnp.concatenate([lefts[i] for i, _ in pairs], contract_left),
        jnp.concatenate([rights[j] for _, j in pairs], 0),
        (((contract_left,), (0,)), ((), ())),
        preferred_element_type=jnp.float32,
    )


def dot_exact(left, right, contract_left):
    return dot_parts(parts_of(left), parts_of(right), contract_left)


def block_pairs(blocks):
    return [(i, j) for i in range(blocks) for j in range(i, blocks)]


def filter_kernel(taps_ref, hours_ref, filtered_ref, gram_ref):
    blocks = hours_ref.shape[0] // BLOCK
    band = pltpu.roll(
        jnp.broadcast_to(taps_ref[...], (BLOCK, 2 * BLOCK)), 0, 1, stride=1, stride_axis=0
    ).astype(jnp.bfloat16)
    for i in range(blocks):
        if i == 0:
            total = jnp.dot(
                band[:, BLOCK:], hours_ref[:BLOCK, :], preferred_element_type=jnp.float32
            )
        else:
            total = jnp.dot(
                band,
                hours_ref[(i - 1) * BLOCK : (i + 1) * BLOCK, :],
                preferred_element_type=jnp.float32,
            )
        filtered_ref[i * BLOCK : (i + 1) * BLOCK, :] = total.astype(jnp.bfloat16)
    place = 0
    for i in range(blocks):
        product = lax.dot_general(
            filtered_ref[i * BLOCK : (i + 1) * BLOCK, :],
            filtered_ref[i * BLOCK :, :],
            (((1,), (1,)), ((), ())),
            preferred_element_type=jnp.float32,
        )
        for j in range(blocks - i):
            gram_ref[place : place + BLOCK, :] = product[:, j * BLOCK : (j + 1) * BLOCK]
            place += BLOCK


def filtered_and_gram(hours, coefs):
    taps = jnp.concatenate(
        [coefs[::-1], jnp.ones((1,), jnp.float32), jnp.zeros((BLOCK - 1,), jnp.float32)]
    )
    count = hours.shape[0]
    pairs = len(block_pairs(count // BLOCK))
    return pl.pallas_call(
        filter_kernel,
        out_shape=[
            jax.ShapeDtypeStruct(hours.shape, jnp.bfloat16),
            jax.ShapeDtypeStruct((pairs * BLOCK, BLOCK), jnp.float32),
        ],
        compiler_params=pltpu.CompilerParams(vmem_limit_bytes=VMEM_BYTES),
    )(taps.reshape(1, 2 * BLOCK), hours)


def eliminate(rows, first):
    tiles = len(rows)
    sublane = lax.broadcasted_iota(jnp.int32, (8, BLOCK), 0)
    lane = lax.broadcasted_iota(jnp.int32, (8, BLOCK), 1) - first
    inside = (lane >= 0) & (lane < PANEL)
    columns = [
        [
            jnp.broadcast_to(rows[t][:, first + k : first + k + 1], (8, BLOCK)) if 8 * t + 8 > k else None
            for t in range(tiles)
        ]
        for k in range(PANEL)
    ]
    rows = [
        jnp.where(inside, (lane == sublane + 8 * t).astype(jnp.float32), rows[t])
        for t in range(tiles)
    ]
    factor = [jnp.zeros((8, BLOCK), jnp.float32) for _ in range(tiles)]
    for j in range(PANEL):
        home, row = divmod(j, 8)
        inverse = lax.rsqrt(columns[j][home][row : row + 1])
        column = [columns[j][t] * inverse if t >= home else None for t in range(tiles)]
        for k in range(j + 1, PANEL):
            if k > j + 1:
                line = column[k // 8][k % 8 : k % 8 + 1]
            else:
                line = columns[j][k // 8][k % 8 : k % 8 + 1] * inverse
            for t in range(k // 8, tiles):
                columns[k][t] = columns[k][t] - column[t] * line
        line = rows[home][row : row + 1] * inverse
        for t in range(home, tiles):
            factor[t] = jnp.where(lane == j, column[t], factor[t])
            if t == home:
                below = jnp.where(sublane > row, column[t], 0.0)
                rows[t] = jnp.where(sublane == row, line, rows[t] - below * line)
            else:
                rows[t] = rows[t] - column[t] * line
    factor = [jnp.where(lane <= sublane + 8 * t, factor[t], 0.0) for t in range(tiles)]
    return rows, factor


def factor_block(work, factor, jobs):
    tiles = PANEL // 8
    lane = lax.broadcasted_iota(jnp.int32, (1, BLOCK), 1)
    for p in range(0, BLOCK, PANEL):
        rows, own = eliminate([work[p + 8 * t : p + 8 * t + 8, :] for t in range(tiles)], p)
        for t in range(tiles):
            work[p + 8 * t : p + 8 * t + 8, :] = rows[t]
            factor[p + 8 * t : p + 8 * t + 8, :] = own[t]
        if p + PANEL < BLOCK:
            panel = parts_of(jnp.concatenate(rows, 0))
            update = dot_parts(panel, panel, 0)[p + PANEL :]
            inside = (lane >= p) & (lane < p + PANEL)
            work[p + PANEL :, :] = jnp.where(inside, 0.0, work[p + PANEL :, :]) - update
        if jobs:
            jobs.pop(0)()


def basis_kernel(
    scale, gram_ref, filtered_ref, basis_ref, lower_ref,
    rest, upper, inverse, work, factor, points, basis, lower, done,
):
    count, width = filtered_ref.shape
    blocks = count // BLOCK
    row = lax.broadcasted_iota(jnp.int32, (BLOCK, BLOCK), 0)
    column = lax.broadcasted_iota(jnp.int32, (BLOCK, BLOCK), 1)
    row, column = row // PANEL, column // PANEL
    for place, (i, j) in enumerate(block_pairs(blocks)):
        rest[i * BLOCK : (i + 1) * BLOCK, j * BLOCK : (j + 1) * BLOCK] = gram_ref[
            place * BLOCK : (place + 1) * BLOCK, :
        ]
    copies, jobs = [], []

    def send(source, target):
        copy = pltpu.make_async_copy(source, target, done.at[len(copies)])
        copy.start()
        copies.append(copy)

    def send_basis(k):
        here = slice(k * BLOCK, (k + 1) * BLOCK)
        send(basis.at[:, here], basis_ref.at[:, here])

    def multiply(left, first, size, k):
        total = None
        for part in left:
            term = lax.dot_general(
                points[first : first + size, : (k + 1) * BLOCK],
                part,
                (((1,), (1,)), ((), ())),
                preferred_element_type=jnp.float32,
            )
            total = term if total is None else total + term
        basis[first : first + size, k * BLOCK : (k + 1) * BLOCK] = total

    for k in range(blocks):
        start, end = k * BLOCK, (k + 1) * BLOCK
        points[:, start:end] = filtered_ref[start:end, :].T
        work[...] = rest[start:end, start:end]
        factor_block(work, factor, jobs)
        while jobs:
            jobs.pop(0)()
        if k > 0:
            send_basis(k - 1)
        corner = jnp.where(row >= column, work[...], 0.0)
        inverse[start:end, start:end] = corner
        corner_parts = parts_of(corner)
        lower[start:end, start:end] = (
            jnp.where(row > column, work[...].T, factor[...]) / scale
        )
        if k + 1 < blocks:
            lower[start:end, end:] = jnp.zeros((BLOCK, count - end), jnp.float32)
            across = dot_parts(corner_parts, parts_of(rest[start:end, end:]), 1)
            across_parts = parts_of(across)
            for i in range(k + 1, blocks):
                first = (i - k - 1) * BLOCK
                rest[i * BLOCK : (i + 1) * BLOCK, i * BLOCK :] = rest[
                    i * BLOCK : (i + 1) * BLOCK, i * BLOCK :
                ] - dot_parts(
                    [part[:, first : first + BLOCK] for part in across_parts],
                    [part[:, first:] for part in across_parts],
                    0,
                )
            upper[start:end, end:] = across
            inverse[start:end, end:] = jnp.zeros((BLOCK, count - end), jnp.float32)
            lower[end:, start:end] = (across / scale).T
        send(lower.at[start:end, :], lower_ref.at[start:end, :])
        if k > 0:
            inner = dot_exact(upper[:start, start:end], inverse[:start, :start], 0)
            inverse[start:end, :start] = -dot_parts(corner_parts, parts_of(inner), 1)
        left = parts_of(inverse[start:end, :end] * scale)
        size = width
        if k + 1 < blocks:
            size = -(-width // (BLOCK // PANEL - 1) // 16) * 16
        jobs = [
            functools.partial(multiply, left, first, min(size, width - first), k)
            for first in range(0, width, size)
        ]
    for job in jobs:
        job()
    send_basis(blocks - 1)
    for copy in copies:
        copy.wait()


def basis_and_factor(gram, filtered, scale):
    count, width = filtered.shape
    square = (count, count)
    anywhere = pl.BlockSpec(memory_space=pl.ANY)
    return pl.pallas_call(
        functools.partial(basis_kernel, scale),
        out_shape=[
            jax.ShapeDtypeStruct((width, count), jnp.float32),
            jax.ShapeDtypeStruct(square, jnp.float32),
        ],
        out_specs=[anywhere, anywhere],
        scratch_shapes=[
            pltpu.VMEM(square, jnp.float32),
            pltpu.VMEM(square, jnp.float32),
            pltpu.VMEM(square, jnp.float32),
            pltpu.VMEM((BLOCK, BLOCK), jnp.float32),
            pltpu.VMEM((BLOCK, BLOCK), jnp.float32),
            pltpu.VMEM((width, count), jnp.bfloat16),
            pltpu.VMEM((width, count), jnp.float32),
            pltpu.VMEM(square, jnp.float32),
            pltpu.SemaphoreType.DMA((2 * (count // BLOCK),)),
        ],
        compiler_params=pltpu.CompilerParams(vmem_limit_bytes=VMEM_BYTES),
    )(gram, filtered)


def split_kernel(hours_ref, parts_ref):
    count, width = hours_ref.shape[0], parts_ref.shape[1]
    for part in range(parts_ref.shape[0] // count):
        parts_ref[part * count : (part + 1) * count, :] = hours_ref[
            :, part * width : (part + 1) * width
        ]


def split_points(hours, parts):
    count, width = hours.shape[0], hours.shape[1] // parts
    return pl.pallas_call(
        split_kernel,
        out_shape=jax.ShapeDtypeStruct((parts * count, width), hours.dtype),
        compiler_params=pltpu.CompilerParams(vmem_limit_bytes=VMEM_BYTES),
    )(hours)


def exchanged(parts, axes):
    return lax.all_to_all(parts, axes, split_axis=0, concat_axis=0, tiled=True)


def scattered_sum(rows, axes):
    count = lax.axis_size(axes)
    return jnp.sum(exchanged(rows, axes).reshape((count, -1) + rows.shape[1:]), 0)


def gathered(piece, axes):
    count = lax.axis_size(axes)
    copies = jnp.broadcast_to(piece[None], (count,) + piece.shape)
    return exchanged(copies.reshape((-1,) + piece.shape[1:]), axes)


def swapped(piece):
    return lax.ppermute(piece, "core", [(0, 1), (1, 0)])


def total_gram(gram):
    core, half = lax.axis_index("core"), gram.shape[0] // 2
    own = lax.dynamic_slice_in_dim(gram, core * half, half)
    other = lax.dynamic_slice_in_dim(gram, (1 - core) * half, half)
    own = (own + swapped(other)).reshape(half // 4, 4, BLOCK)
    piece = scattered_sum(own, ("x", "z"))
    piece = jnp.sum(gathered(piece, "tm").reshape((-1,) + piece.shape), 0)
    own = gathered(piece, ("x", "z")).reshape(half, BLOCK)
    other = swapped(own)
    first = core == 0
    return jnp.concatenate([jnp.where(first, own, other), jnp.where(first, other, own)], 0)


def body(thermal_anomaly, smoothing_coefs):
    points = thermal_anomaly.shape[1] * lax.axis_size(("x", "z", "core"))
    scale = math.sqrt(points)
    hours = exchanged(split_points(thermal_anomaly, lax.axis_size("tm")), "tm")
    filtered, gram = filtered_and_gram(hours, smoothing_coefs)
    basis, lower = basis_and_factor(total_gram(gram), filtered, scale)
    return basis.T, lower


def solution(mesh):
    fine = Mesh(mesh.devices.reshape(4, 8, 2, 8), ("x", "z", "core", "tm"))
    space = ("x", "z", "core")
    return jax.shard_map(
        body,
        mesh=fine,
        in_specs=(P("tm", space), P()),
        out_specs=(P(None, space + ("tm",)), P()),
        check_vma=False,
    )
```

```python
import functools
import math

import jax
import jax.numpy as jnp
from jax import lax
from jax.experimental import pallas as pl
from jax.experimental.pallas import tpu as pltpu
from jax.sharding import Mesh, PartitionSpec as P

BLOCK = 128
PANEL = 16
GROUP = 32
VMEM_BYTES = 48 * 2**20


def parts_of(value):
    found = []
    for _ in range(3):
        part = value.astype(jnp.bfloat16)
        value = value - part.astype(jnp.float32)
        found.append(part)
    return found


def dot_parts(lefts, rights, contract_left):
    pairs = ((0, 0), (0, 1), (1, 0), (0, 2), (2, 0), (1, 1))
    return lax.dot_general(
        jnp.concatenate([lefts[i] for i, _ in pairs], contract_left),
        jnp.concatenate([rights[j] for _, j in pairs], 0),
        (((contract_left,), (0,)), ((), ())),
        preferred_element_type=jnp.float32,
    )


def dot_exact(left, right, contract_left):
    return dot_parts(parts_of(left), parts_of(right), contract_left)


def block_pairs(blocks):
    return [(i, j) for i in range(blocks) for j in range(i, blocks)]


def filter_kernel(taps_ref, hours_ref, filtered_ref, gram_ref):
    blocks = hours_ref.shape[0] // BLOCK
    band = pltpu.roll(
        jnp.broadcast_to(taps_ref[...], (BLOCK, 2 * BLOCK)), 0, 1, stride=1, stride_axis=0
    ).astype(jnp.bfloat16)
    for i in range(blocks):
        if i == 0:
            total = jnp.dot(
                band[:, BLOCK:], hours_ref[:BLOCK, :], preferred_element_type=jnp.float32
            )
        else:
            total = jnp.dot(
                band,
                hours_ref[(i - 1) * BLOCK : (i + 1) * BLOCK, :],
                preferred_element_type=jnp.float32,
            )
        filtered_ref[i * BLOCK : (i + 1) * BLOCK, :] = total.astype(jnp.bfloat16)
    place = 0
    for i in range(blocks):
        product = lax.dot_general(
            filtered_ref[i * BLOCK : (i + 1) * BLOCK, :],
            filtered_ref[i * BLOCK :, :],
            (((1,), (1,)), ((), ())),
            preferred_element_type=jnp.float32,
        )
        for j in range(blocks - i):
            gram_ref[place : place + BLOCK, :] = product[:, j * BLOCK : (j + 1) * BLOCK]
            place += BLOCK


def filtered_and_gram(hours, coefs):
    taps = jnp.concatenate(
        [coefs[::-1], jnp.ones((1,), jnp.float32), jnp.zeros((BLOCK - 1,), jnp.float32)]
    )
    count = hours.shape[0]
    pairs = len(block_pairs(count // BLOCK))
    return pl.pallas_call(
        filter_kernel,
        out_shape=[
            jax.ShapeDtypeStruct(hours.shape, jnp.bfloat16),
            jax.ShapeDtypeStruct((pairs * BLOCK, BLOCK), jnp.float32),
        ],
        compiler_params=pltpu.CompilerParams(vmem_limit_bytes=VMEM_BYTES),
    )(taps.reshape(1, 2 * BLOCK), hours)


def eliminate(rows, first):
    tiles, own = len(rows), PANEL // 8
    sublane = lax.broadcasted_iota(jnp.int32, (8, BLOCK), 0)
    lane = lax.broadcasted_iota(jnp.int32, (8, BLOCK), 1) - first
    inside = (lane >= 0) & (lane < PANEL)
    columns = [
        [
            jnp.broadcast_to(rows[t][:, first + k : first + k + 1], (8, BLOCK)) if 8 * t + 8 > k else None
            for t in range(tiles)
        ]
        for k in range(PANEL)
    ]
    rows = [
        jnp.where(inside, (lane == sublane + 8 * t).astype(jnp.float32), rows[t])
        for t in range(tiles)
    ]
    factor = [jnp.zeros((8, BLOCK), jnp.float32) for _ in range(own)]
    for j in range(PANEL):
        home, row = divmod(j, 8)
        inverse = lax.rsqrt(columns[j][home][row : row + 1])
        column = [columns[j][t] * inverse if t >= home else None for t in range(tiles)]
        for k in range(j + 1, PANEL):
            if k > j + 2:
                line = column[k // 8][k % 8 : k % 8 + 1]
            else:
                line = columns[j][k // 8][k % 8 : k % 8 + 1] * inverse
            for t in range(k // 8, tiles):
                columns[k][t] = columns[k][t] - column[t] * line
        line = rows[home][row : row + 1] * inverse
        for t in range(home, tiles):
            if t < own:
                factor[t] = jnp.where(lane == j, column[t], factor[t])
            if t == home:
                below = jnp.where(sublane > row, column[t], 0.0)
                rows[t] = jnp.where(sublane == row, line, rows[t] - below * line)
            else:
                rows[t] = rows[t] - column[t] * line
    factor = [jnp.where(lane <= sublane + 8 * t, factor[t], 0.0) for t in range(own)]
    return rows, factor


def factor_block(work, factor, jobs):
    tiles = GROUP // 8
    lane = lax.broadcasted_iota(jnp.int32, (1, BLOCK), 1)
    for p in range(0, BLOCK, GROUP):
        rows = [work[p + 8 * t : p + 8 * t + 8, :] for t in range(tiles)]
        sent = []
        for first in range(p, p + GROUP, PANEL):
            rows, own = eliminate(rows, first)
            beyond = (lane >= first + PANEL) & (lane < p + GROUP)
            for t in range(PANEL // 8):
                work[first + 8 * t : first + 8 * t + 8, :] = rows[t]
                factor[first + 8 * t : first + 8 * t + 8, :] = own[t]
                sent.append(jnp.where(beyond, 0.0, rows[t]))
            rows = rows[PANEL // 8 :]
        if p + GROUP < BLOCK:
            panel = parts_of(jnp.concatenate(sent, 0))
            update = dot_parts(panel, panel, 0)[p + GROUP :]
            inside = (lane >= p) & (lane < p + GROUP)
            work[p + GROUP :, :] = jnp.where(inside, 0.0, work[p + GROUP :, :]) - update
        if jobs:
            jobs.pop(0)()


def basis_kernel(
    scale, gram_ref, points, basis_ref, lower_ref,
    rest, upper, inverse, work, factor, basis, lower, done,
):
    width, count = points.shape
    blocks = count // BLOCK
    row = lax.broadcasted_iota(jnp.int32, (BLOCK, BLOCK), 0)
    column = lax.broadcasted_iota(jnp.int32, (BLOCK, BLOCK), 1)
    row, column = row // PANEL, column // PANEL
    for place, (i, j) in enumerate(block_pairs(blocks)):
        rest[i * BLOCK : (i + 1) * BLOCK, j * BLOCK : (j + 1) * BLOCK] = gram_ref[
            place * BLOCK : (place + 1) * BLOCK, :
        ]
    copies, jobs = [], []

    def send(source, target):
        copy = pltpu.make_async_copy(source, target, done.at[len(copies)])
        copy.start()
        copies.append(copy)

    def send_basis(k):
        here = slice(k * BLOCK, (k + 1) * BLOCK)
        send(basis.at[:, here], basis_ref.at[:, here])

    def multiply(left, first, size, k):
        total = None
        for part in left:
            term = lax.dot_general(
                points[first : first + size, : (k + 1) * BLOCK],
                part,
                (((1,), (1,)), ((), ())),
                preferred_element_type=jnp.float32,
            )
            total = term if total is None else total + term
        basis[first : first + size, k * BLOCK : (k + 1) * BLOCK] = total

    for k in range(blocks):
        start, end = k * BLOCK, (k + 1) * BLOCK
        work[...] = rest[start:end, start:end]
        factor_block(work, factor, jobs)
        while jobs:
            jobs.pop(0)()
        if k > 0:
            send_basis(k - 1)
        corner = jnp.where(row >= column, work[...], 0.0)
        inverse[start:end, start:end] = corner
        corner_parts = parts_of(corner)
        lower[start:end, start:end] = (
            jnp.where(row > column, work[...].T, factor[...]) / scale
        )
        if k + 1 < blocks:
            lower[start:end, end:] = jnp.zeros((BLOCK, count - end), jnp.float32)
            across = dot_parts(corner_parts, parts_of(rest[start:end, end:]), 1)
            across_parts = parts_of(across)
            for i in range(k + 1, blocks):
                first = (i - k - 1) * BLOCK
                rest[i * BLOCK : (i + 1) * BLOCK, i * BLOCK :] = rest[
                    i * BLOCK : (i + 1) * BLOCK, i * BLOCK :
                ] - dot_parts(
                    [part[:, first : first + BLOCK] for part in across_parts],
                    [part[:, first:] for part in across_parts],
                    0,
                )
            upper[start:end, end:] = across
            inverse[start:end, end:] = jnp.zeros((BLOCK, count - end), jnp.float32)
            lower[end:, start:end] = (across / scale).T
        send(lower.at[start:end, :], lower_ref.at[start:end, :])
        if k > 0:
            inner = dot_exact(upper[:start, start:end], inverse[:start, :start], 0)
            inverse[start:end, :start] = -dot_parts(corner_parts, parts_of(inner), 1)
        left = parts_of(inverse[start:end, :end] * scale)
        size = width
        if k + 1 < blocks:
            size = -(-width // (BLOCK // GROUP - 1) // 16) * 16
        jobs = [
            functools.partial(multiply, left, first, min(size, width - first), k)
            for first in range(0, width, size)
        ]
    for job in jobs:
        job()
    send_basis(blocks - 1)
    for copy in copies:
        copy.wait()


def turn_kernel(filtered_ref, points_ref):
    for start in range(0, filtered_ref.shape[0], BLOCK):
        points_ref[:, start : start + BLOCK] = filtered_ref[start : start + BLOCK, :].T


def turned(filtered):
    return pl.pallas_call(
        turn_kernel,
        out_shape=jax.ShapeDtypeStruct(filtered.shape[::-1], filtered.dtype),
        compiler_params=pltpu.CompilerParams(vmem_limit_bytes=VMEM_BYTES),
        cost_estimate=pl.CostEstimate(
            flops=0, bytes_accessed=4 * filtered.size, transcendentals=0
        ),
    )(filtered)


def basis_and_factor(gram, points, scale):
    width, count = points.shape
    square = (count, count)
    anywhere = pl.BlockSpec(memory_space=pl.ANY)
    return pl.pallas_call(
        functools.partial(basis_kernel, scale),
        out_shape=[
            jax.ShapeDtypeStruct((width, count), jnp.float32),
            jax.ShapeDtypeStruct(square, jnp.float32),
        ],
        out_specs=[anywhere, anywhere],
        scratch_shapes=[
            pltpu.VMEM(square, jnp.float32),
            pltpu.VMEM(square, jnp.float32),
            pltpu.VMEM(square, jnp.float32),
            pltpu.VMEM((BLOCK, BLOCK), jnp.float32),
            pltpu.VMEM((BLOCK, BLOCK), jnp.float32),
            pltpu.VMEM((width, count), jnp.float32),
            pltpu.VMEM(square, jnp.float32),
            pltpu.SemaphoreType.DMA((2 * (count // BLOCK),)),
        ],
        compiler_params=pltpu.CompilerParams(vmem_limit_bytes=VMEM_BYTES),
    )(gram, points)


def split_kernel(hours_ref, parts_ref):
    count, width = hours_ref.shape[0], parts_ref.shape[1]
    for part in range(parts_ref.shape[0] // count):
        parts_ref[part * count : (part + 1) * count, :] = hours_ref[
            :, part * width : (part + 1) * width
        ]


def split_points(hours, parts):
    count, width = hours.shape[0], hours.shape[1] // parts
    return pl.pallas_call(
        split_kernel,
        out_shape=jax.ShapeDtypeStruct((parts * count, width), hours.dtype),
        compiler_params=pltpu.CompilerParams(vmem_limit_bytes=VMEM_BYTES),
    )(hours)


def exchanged(parts, axes):
    return lax.all_to_all(parts, axes, split_axis=0, concat_axis=0, tiled=True)


def scattered_sum(rows, axes):
    count = lax.axis_size(axes)
    return jnp.sum(exchanged(rows, axes).reshape((count, -1) + rows.shape[1:]), 0)


def gathered(piece, axes):
    count = lax.axis_size(axes)
    copies = jnp.broadcast_to(piece[None], (count,) + piece.shape)
    return exchanged(copies.reshape((-1,) + piece.shape[1:]), axes)


def swapped(piece):
    return lax.ppermute(piece, "core", [(0, 1), (1, 0)])


def total_gram(gram):
    core, half = lax.axis_index("core"), gram.shape[0] // 2
    own = lax.dynamic_slice_in_dim(gram, core * half, half)
    other = lax.dynamic_slice_in_dim(gram, (1 - core) * half, half)
    own = (own + swapped(other)).reshape(half // 4, 4, BLOCK)
    piece = scattered_sum(own, ("x", "z"))
    piece = jnp.sum(gathered(piece, "tm").reshape((-1,) + piece.shape), 0)
    own = gathered(piece, ("x", "z")).reshape(half, BLOCK)
    other = swapped(own)
    first = core == 0
    return jnp.concatenate([jnp.where(first, own, other), jnp.where(first, other, own)], 0)


def body(thermal_anomaly, smoothing_coefs):
    points = thermal_anomaly.shape[1] * lax.axis_size(("x", "z", "core"))
    scale = math.sqrt(points)
    hours = exchanged(split_points(thermal_anomaly, lax.axis_size("tm")), "tm")
    filtered, gram = filtered_and_gram(hours, smoothing_coefs)
    basis, lower = basis_and_factor(total_gram(gram), turned(filtered), scale)
    return basis.T, lower


def solution(mesh):
    fine = Mesh(mesh.devices.reshape(4, 8, 2, 8), ("x", "z", "core", "tm"))
    space = ("x", "z", "core")
    return jax.shard_map(
        body,
        mesh=fine,
        in_specs=(P("tm", space), P()),
        out_specs=(P(None, space + ("tm",)), P()),
        check_vma=False,
    )
```
